32 devices in a mesh: section: 2 (over y), expert: 16 (over z, x, core).
Axes of the slice: x: 2, y: 2, z: 4, core: 2. Of those that a mesh axis runs over, the one named last changes fastest.
Arguments:
- act_fwd: bfloat16 [2, 2048, 4096], P('section', 'expert'), may hold values from -6 to 6
- act_rev: bfloat16 [2, 2048, 4096], P('section', 'expert'), may hold values from -6 to 6
- ids_fwd: int32 [2, 2048, 2], P('section', 'expert'), may hold values from 0 to 7, all different within a row; in each aligned block of 128 rows (0 to 127, 128 to 255, ..., all dimensions but the last counted through in order) at most 48 rows name the same one
- ids_rev: int32 [2, 2048, 2], P('section', 'expert'), may hold values from 0 to 7, all different within a row; in each aligned block of 128 rows (0 to 127, 128 to 255, ..., all dimensions but the last counted through in order) at most 48 rows name the same one
- probs_fwd: float32 [2, 2048, 2], P('section', 'expert'), may hold values from 0.05 to 1
- probs_rev: float32 [2, 2048, 2], P('section', 'expert'), may hold values from 0.05 to 1
- w_gate: bfloat16 [2, 4096, 6144], P('section', None, 'expert'), may hold values from -0.09375 to 0.09375
- w_up: bfloat16 [2, 4096, 6144], P('section', None, 'expert'), may hold values from -0.09375 to 0.09375
- w_down: bfloat16 [2, 6144, 4096], P('section', 'expert'), may hold values from -0.21875 to 0.21875
Outputs:
- out_fwd: bfloat16 [2, 2048, 4096], P('section', 'expert')
- out_rev: bfloat16 [2, 2048, 4096], P('section', 'expert')
The draws below stay inside these ranges and needn't reach their ends.
Inputs may be any that keep to these rules, and one draw needn't show every extreme that they name: `ids_fwd`: each row names 2 different experts. Within the 128 rows of one device (aligned blocks) no expert is named by more than 48 rows, and some block reaches 48. `ids_rev`: as for ids_fwd.
All inputs are finite; a program needn't handle non-finite values.
Results may differ from the reference program's by a relative error of at most 0.0048.
Values may be sent and summed in bfloat16 or wider, within the bound.
A program may use at most 128 MiB of HBM per device.

```python
import math
import jax
import jax.numpy as jnp
import numpy as np
from jax import lax

D = 4096
HID = 768
TOPK = 2
TOK = 128
HALF = 384
SECTIONS = 2
EXPERTS = 8
TOKENS = 2048
CAP = 48
N_EXPERT = 16


def levels(key, shape, cuts, smallest, largest):
    def one(dim, blocks):
        steps = jax.random.uniform(jax.random.fold_in(jax.random.fold_in(key, 6), dim), (blocks,), jnp.float32, smallest / len(cuts), largest / len(cuts))
        return jnp.repeat(jnp.exp(steps), shape[dim] // blocks).reshape((-1,) + (1,) * (len(shape) - dim - 1))

    level = one(*cuts[0])
    for cut in cuts[1:]:
        level = level * one(*cut)
    return level


def deal_out(stream_key, own, number, rows, count, top, most, slope):
    sequence = jax.random.permutation(stream_key, count)
    crowded, ordinary = shares(count, rows * top, most, slope, True), shares(count, rows * top, most, slope, False)
    places = jnp.arange(count)

    def named(lengths, turn):
        used = int((lengths > 0).sum())
        fixed = max(1, used // 4)
        passed = fixed + (places - fixed + turn * (used - fixed)) % max(1, count - fixed)
        return jnp.zeros((count,), jnp.int32).at[sequence[jnp.where(places < fixed, places, passed)]].set(jnp.asarray(lengths, jnp.int32))

    lengths = jnp.where(number % 4 == 0, named(crowded, number // 4), named(ordinary, number - number // 4 - 1))
    mixed = jax.random.permutation(jax.random.fold_in(own, 3), count)
    donor, taker = mixed[0:count // 2 * 2:2], mixed[1:count // 2 * 2:2]
    slack = jnp.minimum(lengths[donor] - 1, most - lengths[taker]) // 2
    slack = jnp.where((donor == sequence[0]) | (taker == sequence[0]) | (lengths[taker] == 0), 0, jnp.maximum(slack, 0))
    passed = jax.random.randint(jax.random.fold_in(own, 4), (count // 2,), 0, 1 << 20) % (slack + 1)
    lengths = lengths.at[donor].add(-passed).at[taker].add(passed)
    members = jnp.searchsorted(jnp.cumsum(lengths), jnp.arange(rows * top), side="right").astype(jnp.int32)
    grid = members.reshape(top, rows).T
    grid = grid[jax.random.permutation(jax.random.fold_in(own, 1), rows)]
    turn = jax.random.randint(jax.random.fold_in(own, 2), (rows, 1), 0, top)
    return jnp.take_along_axis(grid, (jnp.arange(top)[None, :] + turn) % top, axis=1)


def shares(count, total, bound, skew, full):
    weights = [(1 << 20) // math.isqrt(rank ** skew) + 1 for rank in range(1, count + 1)]
    largest = bound if full else min(bound, max(-(-total // count), total * weights[0] // sum(weights)))
    least = 1 if total - largest >= count - 1 else 0
    given, spare = [largest] + [least] * (count - 1), total - largest - least * (count - 1)
    while spare > 0:
        free = [i for i in range(1, count) if given[i] < largest] or [i for i in range(1, count) if given[i] < bound]
        pool, left = sum([weights[i] for i in free]), spare
        for i in free:
            more = min(bound - given[i], max(1, left * weights[i] // pool), spare)
            given[i] = given[i] + more
            spare = spare - more
    return np.array(given)


def noise(rng, dims, scale, reach, split=(), kind=jnp.bfloat16):
    drawn = scale * jax.random.normal(rng, dims, jnp.float32)
    if split:
        drawn = drawn * levels(rng, dims, split, -0.22, 0.18)
    return jnp.clip(drawn, -reach, reach).astype(kind)


def setup_inputs(seed: int = 0) -> dict:
    key_list = jax.random.split(jax.random.key(seed), 10)
    act_fwd = noise(key_list[0], (SECTIONS, TOKENS, D), 1.0, 6.0, ((0, 2), (1, 16)))
    act_rev = noise(key_list[1], (SECTIONS, TOKENS, D), 1.0, 6.0, ((0, 2), (1, 16)))
    ids_fwd_keys = jax.random.split(jax.random.fold_in(key_list[2], 1), SECTIONS * TOKENS // TOK)
    ids_fwd_turns = jax.random.permutation(jax.random.fold_in(key_list[2], 3), SECTIONS * TOKENS // TOK)
    ids_fwd = jax.vmap(lambda own, number: deal_out(jax.random.fold_in(key_list[2], 2), own, number, TOK, EXPERTS, TOPK, CAP, 2))(ids_fwd_keys, ids_fwd_turns).reshape((SECTIONS, TOKENS, TOPK))
    ids_rev_keys = jax.random.split(jax.random.fold_in(key_list[3], 1), SECTIONS * TOKENS // TOK)
    ids_rev_turns = jax.random.permutation(jax.random.fold_in(key_list[3], 3), SECTIONS * TOKENS // TOK)
    ids_rev = jax.vmap(lambda own, number: deal_out(jax.random.fold_in(key_list[3], 2), own, number, TOK, EXPERTS, TOPK, CAP, 2))(ids_rev_keys, ids_rev_turns).reshape((SECTIONS, TOKENS, TOPK))
    probs_fwd = jnp.clip(jnp.exp(math.log(1.0) - 2.9957323 * jax.random.uniform(key_list[4], (SECTIONS, TOKENS, TOPK), jnp.float32) ** levels(key_list[4], (SECTIONS, TOKENS, TOPK), ((0, 2), (1, 16)), -0.2, 0.2)), 0.05, 1.0)
    probs_rev = jnp.clip(jnp.exp(math.log(1.0) - 2.9957323 * jax.random.uniform(key_list[5], (SECTIONS, TOKENS, TOPK), jnp.float32) ** levels(key_list[5], (SECTIONS, TOKENS, TOPK), ((0, 2), (1, 16)), -0.2, 0.2)), 0.05, 1.0)
    w_gate = noise(key_list[6], (SECTIONS, D, EXPERTS * HID), D ** -0.5, 0.09375, ((0, 2), (2, 16)))
    w_up = noise(key_list[7], (SECTIONS, D, EXPERTS * HID), D ** -0.5, 0.09375, ((0, 2), (2, 16)))
    w_down = noise(key_list[8], (SECTIONS, EXPERTS * HID, D), HID ** -0.5, 0.21875, ((0, 2), (1, 16)))
    return dict(act_fwd=act_fwd, act_rev=act_rev, ids_fwd=ids_fwd, ids_rev=ids_rev, probs_fwd=probs_fwd, probs_rev=probs_rev, w_gate=w_gate, w_up=w_up, w_down=w_down)


def expert_apply(chosen, w_gate_s, w_up_s, w_down_s, expert_id):
    pieces = []
    for half_id in range(2):
        start = (expert_id * HID + half_id * HALF).astype(jnp.int32)
        gate_cols = lax.dynamic_slice_in_dim(w_gate_s, start, HALF, 1)
        up_cols = lax.dynamic_slice_in_dim(w_up_s, start, HALF, 1)
        down_rows = lax.dynamic_slice_in_dim(w_down_s, start, HALF, 0)
        gate_pre = jnp.dot(chosen, gate_cols, preferred_element_type=jnp.float32)
        up_pre = jnp.dot(chosen, up_cols, preferred_element_type=jnp.float32)
        hidden = (jax.nn.silu(gate_pre) * up_pre).astype(jnp.bfloat16)
        partial_value = jnp.dot(hidden, down_rows, preferred_element_type=jnp.float32).astype(jnp.bfloat16)
        pieces.append(partial_value.astype(jnp.float32))
    return (pieces[0] + pieces[1]).astype(jnp.bfloat16)


def moe_layer(tokens_in, route_ids, probs, w_gate_s, w_up_s, w_down_s):
    route_total = TOKENS * TOPK
    slot_total = N_EXPERT * CAP
    flat_ids = route_ids.reshape(-1).astype(jnp.int32)
    weights = probs / jnp.sum(probs, axis=1, keepdims=True)

    def one_expert(accumulated, expert_id):
        is_this = flat_ids == expert_id
        rank_in = jnp.cumsum(is_this.astype(jnp.int32)) - 1
        placed_at = jnp.where(is_this, rank_in, slot_total).astype(jnp.int32)
        slot_index = jnp.zeros((slot_total,), jnp.int32).at[placed_at].set(jnp.arange(route_total, dtype=jnp.int32), mode="drop")
        slot_used = jnp.zeros((slot_total,), jnp.float32).at[placed_at].set(1.0, mode="drop")
        chosen = tokens_in[slot_index // TOPK]
        result = expert_apply(chosen, w_gate_s, w_up_s, w_down_s, expert_id).astype(jnp.float32)
        accumulated = accumulated.at[slot_index].add(result * slot_used[:, None])
        return accumulated, None

    start_sum = jnp.zeros((route_total, D), jnp.float32)
    accumulated, unused = lax.scan(one_expert, start_sum, jnp.arange(EXPERTS, dtype=jnp.int32))
    per_route = accumulated.reshape(TOKENS, TOPK, D)
    mixed = tokens_in.astype(jnp.float32) + jnp.sum(per_route * weights[:, :, None], axis=1)
    return mixed.astype(jnp.bfloat16)


def reference(act_fwd, act_rev, ids_fwd, ids_rev, probs_fwd, probs_rev, w_gate, w_up, w_down):
    arrived_fwd = jnp.roll(act_fwd, 1, axis=0)
    arrived_rev = jnp.roll(act_rev, -1, axis=0)
    forward_list = []
    reverse_list = []
    for section_id in range(SECTIONS):
        forward_list.append(moe_layer(arrived_fwd[section_id], ids_fwd[section_id], probs_fwd[section_id], w_gate[section_id], w_up[section_id], w_down[section_id]))
        reverse_list.append(moe_layer(arrived_rev[section_id], ids_rev[section_id], probs_rev[section_id], w_gate[section_id], w_up[section_id], w_down[section_id]))
    return (jnp.stack(forward_list), jnp.stack(reverse_list))
```

```python
import jax
import jax.numpy as jnp
from jax import lax
from jax.sharding import PartitionSpec as P


def from_behind(block, axis, distance):
    devices = range(lax.axis_size(axis))
    route = [((i - distance) % len(devices), i) for i in devices]
    return lax.ppermute(block, axis, route)


def from_core(block):
    devices = range(lax.axis_size("expert"))
    return lax.ppermute(block, "expert", [(i, i + 1 - 2 * (i % 2)) for i in devices])


def half_expert(rows, w_gate, w_up, w_down):
    gate_pre = jnp.dot(rows, w_gate, preferred_element_type=jnp.float32)
    up_pre = jnp.dot(rows, w_up, preferred_element_type=jnp.float32)
    hidden = (jax.nn.silu(gate_pre) * up_pre).astype(jnp.bfloat16)
    return jnp.dot(hidden, w_down, preferred_element_type=jnp.float32).astype(jnp.bfloat16)


def moe_layer(tokens_in, route_ids, probs, weights_here, weights_there):
    tok_count, route_count = route_ids.shape
    model_width = tokens_in.shape[1]
    device_count = lax.axis_size("expert")
    expert_count = device_count // 2
    groups = [list(range(0, device_count, 2)), list(range(1, device_count, 2))]
    slot_count = 2 * (3 * tok_count * route_count // (4 * expert_count))
    flat_ids = route_ids.reshape(-1)
    one_hot = (flat_ids[:, None] == jnp.arange(expert_count, dtype=jnp.int32)[None, :]).astype(
        jnp.int32
    )
    rank_in = jnp.sum((jnp.cumsum(one_hot, axis=0) - 1) * one_hot, axis=1)
    slot_of = flat_ids * slot_count + rank_in
    slot_range = jnp.arange(expert_count * slot_count, dtype=jnp.int32)
    pick_rows = (slot_range[:, None] == slot_of[None, :]).astype(jnp.bfloat16)
    pick_tokens = jnp.sum(
        pick_rows.reshape(expert_count * slot_count, tok_count, route_count), axis=2
    )
    outgoing = jnp.dot(pick_tokens, tokens_in, preferred_element_type=jnp.float32).astype(
        jnp.bfloat16
    )
    received = lax.all_to_all(
        outgoing.reshape(expert_count, slot_count, model_width),
        "expert", split_axis=0, concat_axis=0, tiled=True, axis_index_groups=groups,
    ).reshape(-1, model_width)
    here = half_expert(received, *weights_here)
    there = half_expert(received, *weights_there)
    expert_sum = (here.astype(jnp.float32) + there.astype(jnp.float32)).astype(jnp.bfloat16)
    expert_out = lax.all_to_all(
        expert_sum.reshape(expert_count, slot_count, model_width),
        "expert", split_axis=0, concat_axis=0, tiled=True, axis_index_groups=groups,
    ).reshape(-1, model_width)
    route_pick = (slot_of[:, None] == slot_range[None, :]).astype(jnp.bfloat16)
    per_route = jnp.dot(route_pick, expert_out, preferred_element_type=jnp.float32)
    weights = probs / jnp.sum(probs, axis=1, keepdims=True)
    mixed = tokens_in.astype(jnp.float32) + jnp.sum(
        per_route.reshape(tok_count, route_count, model_width) * weights[:, :, None], axis=1
    )
    return mixed.astype(jnp.bfloat16)


def body(act_fwd, act_rev, ids_fwd, ids_rev, probs_fwd, probs_rev, w_gate, w_up, w_down):
    here = (w_gate[0], w_up[0], w_down[0])
    arrived_fwd = from_behind(act_fwd, "section", 1)
    there = tuple(from_core(w) for w in here)
    arrived_rev = from_behind(act_rev, "section", -1)
    out_fwd = moe_layer(arrived_fwd[0], ids_fwd[0], probs_fwd[0], here, there)
    out_rev = moe_layer(arrived_rev[0], ids_rev[0], probs_rev[0], here, there)
    return (out_fwd[None], out_rev[None])


def solution(mesh):
    return jax.shard_map(
        body,
        mesh=mesh,
        in_specs=(
            P("section", "expert", None),
            P("section", "expert", None),
            P("section", "expert", None),
            P("section", "expert", None),
            P("section", "expert", None),
            P("section", "expert", None),
            P("section", None, "expert"),
            P("section", None, "expert"),
            P("section", "expert", None),
        ),
        out_specs=(P("section", "expert", None), P("section", "expert", None)),
        check_vma=False,
    )
```

```python
import functools

import jax
import jax.numpy as jnp
from jax import lax
from jax.experimental import pallas as pl
from jax.experimental.pallas import tpu as pltpu
from jax.sharding import PartitionSpec as P

MESH = pl.DeviceIdType.MESH
F32 = jnp.float32
BF16 = jnp.bfloat16


def kernel(
    sections, nh, slots, width,
    act_f, act_r, meta_here, w_gate, w_up, w_down,
    out_f, out_r,
    wg, wu, wd, meta_there, arrived, raw, outgoing, received, returned, part, pick, comb,
    acc_g, acc_u, hidden,
    w_local, w_send, w_recv, meta_send, meta_recv, relay_send, relay_recv, raw_send, raw_recv,
    disp_send, disp_recv, ret_send, ret_recv, part_send, part_recv,
):
    half_units = w_gate.shape[-1]
    tokens = arrived.shape[2]
    section = lax.axis_index("section")
    me = lax.axis_index("expert")
    core = lax.rem(me, 2)
    chip = me // 2
    half = chip // nh
    loc = lax.rem(chip, nh)

    def in_half(offset):
        return (section, (half * nh + lax.rem(loc + offset + nh, nh)) * 2 + core)

    partner = (section, lax.rem(chip + nh, 2 * nh) * 2 + core)
    other_core = (section, chip * 2 + 1 - core)
    after = (lax.rem(section + 1, sections), me)
    before = (lax.rem(section + sections - 1, sections), me)
    acts, outs, ways = (act_f, act_r), (out_f, out_r), (after, before)

    def columns(c):
        return pl.ds(pl.multiple_of(c * width, width), width)

    def remote(src, dst, send, recv, device):
        return pltpu.make_async_remote_copy(
            src_ref=src, dst_ref=dst, send_sem=send, recv_sem=recv,
            device_id=device, device_id_type=MESH,
        )

    def relay(st, c):
        return remote(acts[st].at[0, :, columns(c)], arrived.at[st, c],
                      relay_send.at[st, c], relay_recv.at[st, c], ways[st])

    def to_proxy(st, c):
        return remote(arrived.at[st, c], raw.at[st, c],
                      raw_send.at[st, c], raw_recv.at[st, c], partner)

    def dispatch(st, p, c, k):
        return remote(outgoing.at[st, p, c, k], received.at[st, c, k, pl.ds(p * slots, slots)],
                      disp_send.at[st, p, c, k], disp_recv.at[st, p, c, k], in_half(k))

    def give_back(st, p, c, k):
        return remote(received.at[st, c, k, pl.ds(p * slots, slots)], returned.at[st, p, c, k],
                      ret_send.at[st, p, c, k], ret_recv.at[st, p, c, k], in_half(-k))

    def from_proxy(st, c):
        return remote(raw.at[st, c], part.at[st, c],
                      part_send.at[st, c], part_recv.at[st, c], partner)

    meta_copy = remote(meta_here, meta_there, meta_send, meta_recv, partner)

    barrier = pltpu.get_barrier_semaphore()
    greeted = [after, before, partner, other_core] + [in_half(k) for k in range(1, nh)]
    for device in greeted:
        pl.semaphore_signal(barrier, inc=1, device_id=device, device_id_type=MESH)
    pl.semaphore_wait(barrier, len(greeted))

    meta_copy.start()

    @pl.loop(0, nh)
    def _(c):
        relay(0, c).start()

    here, there = pl.ds(0, half_units), pl.ds(half_units, half_units)
    places = ((w_gate, wg.at[:, here], wg.at[:, there]), (w_up, wu.at[:, here], wu.at[:, there]),
              (w_down, wd.at[here, :], wd.at[there, :]))
    local_copies, core_copies = [], []
    for i, (w, mine, theirs) in enumerate(places):
        local_copies.append(pltpu.make_async_copy(w.at[0], mine, w_local.at[i]))
        core_copies.append(remote(w.at[0], theirs, w_send.at[i], w_recv.at[i], other_core))
        local_copies[i].start()
        core_copies[i].start()

    row = lax.broadcasted_iota(jnp.int32, (tokens, tokens), 0)
    col = lax.broadcasted_iota(jnp.int32, (tokens, tokens), 1)
    earlier = jnp.where(row < col, 1.0, 0.0).astype(BF16)
    turn = loc + lax.broadcasted_iota(jnp.int32, (8, tokens), 0)
    expert = (half * nh + jnp.where(turn >= nh, turn - nh, turn)).astype(F32)
    slot_id = lax.broadcasted_iota(jnp.int32, (slots, tokens), 0).astype(F32)

    def tables(meta, p):
        for st in range(2):
            i0, i1 = meta[2 * st:2 * st + 1, :], meta[2 * st + 1:2 * st + 2, :]
            p0, p1 = meta[4 + 2 * st:5 + 2 * st, :], meta[5 + 2 * st:6 + 2 * st, :]
            total = p0 + p1
            first, second = i0 == expert, i1 == expert
            named = jnp.where(first, 1.0, jnp.where(second, 1.0, 0.0))
            gate = jnp.where(first, p0 / total, jnp.where(second, p1 / total, 0.0))
            rank = jnp.dot(named.astype(BF16), earlier, preferred_element_type=F32)
            slot = jnp.where(named > 0.5, rank, -1.0)
            weighted = []
            for k in range(nh):
                chosen = jnp.where(slot_id == slot[k:k + 1, :], 1.0, 0.0)
                pick[st, p, pl.ds(k * slots, slots), :] = chosen.astype(BF16)
                weighted.append(chosen * gate[k:k + 1, :])
            flat = jnp.concatenate(weighted, axis=0).T
            top = flat.astype(BF16)
            comb[st, p, 0] = top
            comb[st, p, 1] = (flat - top.astype(F32)).astype(BF16)

    def send_rows(st, p, c, tokens_ref):
        rows = jnp.dot(pick[st, p], tokens_ref[st, c], preferred_element_type=F32).astype(BF16)
        received[st, c, 0, pl.ds(p * slots, slots), :] = rows[:slots]
        for k in range(1, nh):
            outgoing[st, p, c, k] = rows[k * slots:(k + 1) * slots]
            dispatch(st, p, c, k).start()

    def own(st, c):
        relay(st, c).wait_recv()
        to_proxy(st, c).start()
        send_rows(st, 0, c, arrived)

    def proxied(st, c):
        to_proxy(st, c).wait_recv()
        send_rows(st, 1, c, raw)

    def experts(st, k):
        acc_g[...] = jnp.zeros_like(acc_g)
        acc_u[...] = jnp.zeros_like(acc_u)

        @pl.loop(0, nh)
        def _(c):
            @pl.when(k > 0)
            def _():
                dispatch(st, 0, c, k).wait_recv()
                dispatch(st, 1, c, k).wait_recv()

            x = received[st, c, k]
            acc_g[...] += jnp.dot(x, wg[columns(c), :], preferred_element_type=F32)
            acc_u[...] += jnp.dot(x, wu[columns(c), :], preferred_element_type=F32)

        g = acc_g[...]
        hidden[...] = (g / (1.0 + jnp.exp(-g)) * acc_u[...]).astype(BF16)

        @pl.loop(0, nh)
        def _(c):
            y = jnp.dot(hidden[...], wd[:, columns(c)], preferred_element_type=F32).astype(BF16)

            @pl.when(k == 0)
            def _():
                returned[st, 0, c, 0] = y[:slots]
                returned[st, 1, c, 0] = y[slots:]

            @pl.when(k > 0)
            def _():
                received[st, c, k] = y
                give_back(st, 1, c, k).start()
                give_back(st, 0, c, k).start()

    def weighted_sum(st, p, c):
        @pl.loop(1, nh)
        def _(k):
            give_back(st, p, c, k).wait_recv()

        rows = returned[st, p, c].reshape(nh * slots, width)
        return (jnp.dot(comb[st, p, 0], rows, preferred_element_type=F32)
                + jnp.dot(comb[st, p, 1], rows, preferred_element_type=F32))

    def proxy_sum(st, c):
        raw[st, c] = weighted_sum(st, 1, c).astype(BF16)
        from_proxy(st, c).start()

    def finish(st, c):
        total = arrived[st, c].astype(F32) + weighted_sum(st, 0, c)
        from_proxy(st, c).wait_recv()
        outs[st][0, :, columns(c)] = (total + part[st, c].astype(F32)).astype(BF16)

    tables(meta_here[...], 0)
    meta_copy.wait_recv()
    tables(meta_there[...], 1)

    @pl.loop(0, nh)
    def _(c):
        own(0, c)
        relay(1, c).start()

    @pl.loop(0, nh)
    def _(c):
        own(1, c)
        proxied(0, c)

    for i in range(3):
        local_copies[i].wait()
        core_copies[i].wait_recv()

    @pl.loop(0, nh)
    def _(c):
        experts(0, c)
        proxied(1, c)

    @pl.loop(0, nh)
    def _(c):
        experts(1, c)
        proxy_sum(0, c)

    @pl.loop(0, nh)
    def _(c):
        proxy_sum(1, c)
        finish(0, c)

    @pl.loop(0, nh)
    def _(c):
        finish(1, c)

    meta_copy.wait_send()
    for i in range(3):
        core_copies[i].wait_send()

    @pl.loop(0, nh)
    def _(c):
        for st in range(2):
            relay(st, c).wait_send()
            to_proxy(st, c).wait_send()
            from_proxy(st, c).wait_send()
            for p in range(2):
                for k in range(1, nh):
                    dispatch(st, p, c, k).wait_send()
                    give_back(st, p, c, k).wait_send()


def body(act_fwd, act_rev, ids_fwd, ids_rev, probs_fwd, probs_rev, w_gate, w_up, w_down):
    tokens, top = ids_fwd.shape[1:]
    model = act_fwd.shape[2]
    units = w_gate.shape[2]
    experts = lax.axis_size("expert") // 2
    nh = experts // 2
    width = model // nh
    cap = 2 * (3 * tokens * top // (4 * experts))
    slots = -(-cap // 16) * 16
    meta = jnp.concatenate(
        [ids_fwd[0].astype(F32), ids_rev[0].astype(F32), probs_fwd[0], probs_rev[0]], axis=1
    ).T
    anywhere = pl.BlockSpec(memory_space=pl.ANY)
    vmem = pl.BlockSpec(memory_space=pltpu.VMEM)
    dma = pltpu.SemaphoreType.DMA
    out = jax.ShapeDtypeStruct((1, tokens, model), BF16)
    return pl.pallas_call(
        functools.partial(kernel, lax.axis_size("section"), nh, slots, width),
        out_shape=(out, out),
        in_specs=[anywhere, anywhere, vmem, anywhere, anywhere, anywhere],
        out_specs=(vmem, vmem),
        scratch_shapes=[
            pltpu.VMEM((model, 2 * units), BF16),
            pltpu.VMEM((model, 2 * units), BF16),
            pltpu.VMEM((2 * units, model), BF16),
            pltpu.VMEM((8, tokens), F32),
            pltpu.VMEM((2, nh, tokens, width), BF16),
            pltpu.VMEM((2, nh, tokens, width), BF16),
            pltpu.VMEM((2, 2, nh, nh, slots, width), BF16),
            pltpu.VMEM((2, nh, nh, 2 * slots, width), BF16),
            pltpu.VMEM((2, 2, nh, nh, slots, width), BF16),
            pltpu.VMEM((2, nh, tokens, width), BF16),
            pltpu.VMEM((2, 2, nh * slots, tokens), BF16),
            pltpu.VMEM((2, 2, 2, tokens, nh * slots), BF16),
            pltpu.VMEM((2 * slots, 2 * units), F32),
            pltpu.VMEM((2 * slots, 2 * units), F32),
            pltpu.VMEM((2 * slots, 2 * units), BF16),
            dma((3,)), dma((3,)), dma((3,)), dma, dma,
            dma((2, nh)), dma((2, nh)), dma((2, nh)), dma((2, nh)),
            dma((2, 2, nh, nh)), dma((2, 2, nh, nh)), dma((2, 2, nh, nh)), dma((2, 2, nh, nh)),
            dma((2, nh)), dma((2, nh)),
        ],
        compiler_params=pltpu.CompilerParams(
            collective_id=0, has_side_effects=True, vmem_limit_bytes=63 * 1024 * 1024
        ),
        cost_estimate=pl.CostEstimate(
            flops=12 * experts * cap * model * 2 * units,
            bytes_accessed=12 * model * units + 8 * tokens * model,
            transcendentals=0,
        ),
    )(act_fwd, act_rev, meta, w_gate, w_up, w_down)


def solution(mesh):
    return jax.shard_map(
        body,
        mesh=mesh,
        in_specs=(
            P("section", "expert", None),
            P("section", "expert", None),
            P("section", "expert", None),
            P("section", "expert", None),
            P("section", "expert", None),
            P("section", "expert", None),
            P("section", None, "expert"),
            P("section", None, "expert"),
            P("section", "expert", None),
        ),
        out_specs=(P("section", "expert", None), P("section", "expert", None)),
        check_vma=False,
    )
```

```python
import functools

import jax
import jax.numpy as jnp
from jax import lax
from jax.experimental import pallas as pl
from jax.experimental.pallas import tpu as pltpu
from jax.sharding import PartitionSpec as P

MESH = pl.DeviceIdType.MESH
F32 = jnp.float32
BF16 = jnp.bfloat16


def kernel(
    sections, nh, slots, width,
    act_f, act_r, meta_here, w_gate, w_up, w_down,
    out_f, out_r,
    wg, wu, wd, meta_there, arrived, raw, out_own, out_proxy, received, returned, part, pick, comb,
    acc_g, acc_u, hidden,
    w_local, w_send, w_recv, meta_send, meta_recv, relay_send, relay_recv, raw_send, raw_recv,
    disp_send, disp_recv, ret_send, ret_recv, part_send, part_recv,
):
    half_units = w_gate.shape[-1]
    tokens = arrived.shape[2]
    nq = nh // 2
    section = lax.axis_index("section")
    me = lax.axis_index("expert")
    core = lax.rem(me, 2)
    chip = me // 2
    half = chip // nh
    loc = lax.rem(chip, nh)
    pos = lax.rem(loc, nq)
    mid = (loc // nq) == (1 - half)
    my_q = jnp.where(mid, 0, 1)
    first_mid = nq * (1 - half)

    def at_chip(c):
        return (section, c * 2 + core)

    def in_half(offset):
        return at_chip(half * nh + lax.rem(loc + offset + nh, nh))

    def mid_peer(j):
        return at_chip(half * nh + first_mid + j)

    proxy = at_chip((1 - half) * nh + nq * half + pos)
    sources = (proxy, at_chip((1 - half) * nh + nq * (1 - half) + pos))
    other_core = (section, chip * 2 + 1 - core)
    after = (lax.rem(section + 1, sections), me)
    before = (lax.rem(section + sections - 1, sections), me)
    acts, outs, ways = (act_f, act_r), (out_f, out_r), (after, before)

    def columns(c):
        return pl.ds(pl.multiple_of(c * width, width), width)

    def remote(src, dst, send, recv, device):
        return pltpu.make_async_remote_copy(
            src_ref=src, dst_ref=dst, send_sem=send, recv_sem=recv,
            device_id=device, device_id_type=MESH,
        )

    def relay(st, c):
        return remote(acts[st].at[0, :, columns(c)], arrived.at[st, c],
                      relay_send.at[st, c], relay_recv.at[st, c], ways[st])

    def to_proxy(st, c, q):
        return remote(arrived.at[st, c], raw.at[st, q, c],
                      raw_send.at[st, c], raw_recv.at[st, q, c], proxy)

    def send_own(st, c, k):
        return remote(out_own.at[st, c, k], received.at[st, 0, c, k],
                      disp_send.at[st, 0, c, k], disp_recv.at[st, 0, c, k], in_half(k))

    def send_proxied(st, q, c, k, block):
        return remote(out_proxy.at[q, c, k], received.at[st, 1, c, block],
                      disp_send.at[st, 1 + q, c, k], disp_recv.at[st, 1, c, block], in_half(k))

    def return_own(st, c, k):
        return remote(received.at[st, 0, c, k], returned.at[st, 0, c, k],
                      ret_send.at[st, 0, c, k], ret_recv.at[st, 0, c, k], in_half(-k))

    def return_proxied(st, q, c, j, k):
        block = 2 * j + q
        return remote(received.at[st, 1, c, block], returned.at[st, 1 + q, c, k],
                      ret_send.at[st, 1, c, block], ret_recv.at[st, 1 + q, c, k], mid_peer(j))

    def from_proxy(st, q, c):
        return remote(raw.at[st, q, c], part.at[st, c],
                      part_send.at[st, q, c], part_recv.at[st, c], sources[q])

    def meta_copy(q):
        return remote(meta_here, meta_there.at[q], meta_send, meta_recv.at[q], proxy)

    barrier = pltpu.get_barrier_semaphore()
    greeted = [after, before, proxy, other_core] + [in_half(k) for k in range(1, nh)]
    for device in greeted:
        pl.semaphore_signal(barrier, inc=1, device_id=device, device_id_type=MESH)

    @pl.when(mid)
    def _():
        for device in sources:
            pl.semaphore_signal(barrier, inc=1, device_id=device, device_id_type=MESH)

    pl.semaphore_wait(barrier, len(greeted) + jnp.where(mid, 2, 0))

    @pl.loop(0, nh)
    def _(c):
        relay(0, c).start()

    meta_copy(my_q).start()

    here, there = pl.ds(0, half_units), pl.ds(half_units, half_units)
    places = ((w_gate, wg.at[:, here], wg.at[:, there]), (w_up, wu.at[:, here], wu.at[:, there]),
              (w_down, wd.at[here, :], wd.at[there, :]))
    local_copies, core_copies = [], []
    for i, (w, mine, theirs) in enumerate(places):
        local_copies.append(pltpu.make_async_copy(w.at[0], mine, w_local.at[i]))
        core_copies.append(remote(w.at[0], theirs, w_send.at[i], w_recv.at[i], other_core))
        local_copies[i].start()
        core_copies[i].start()

    row = lax.broadcasted_iota(jnp.int32, (tokens, tokens), 0)
    col = lax.broadcasted_iota(jnp.int32, (tokens, tokens), 1)
    earlier = jnp.where(row < col, 1.0, 0.0).astype(BF16)
    turn = loc + lax.broadcasted_iota(jnp.int32, (8, tokens), 0)
    expert = (half * nh + jnp.where(turn >= nh, turn - nh, turn)).astype(F32)
    slot_id = lax.broadcasted_iota(jnp.int32, (slots, tokens), 0).astype(F32)

    def tables(meta, p):
        for st in range(2):
            i0, i1 = meta[2 * st:2 * st + 1, :], meta[2 * st + 1:2 * st + 2, :]
            p0, p1 = meta[4 + 2 * st:5 + 2 * st, :], meta[5 + 2 * st:6 + 2 * st, :]
            total = p0 + p1
            first, second = i0 == expert, i1 == expert
            named = jnp.where(first, 1.0, jnp.where(second, 1.0, 0.0))
            gate = jnp.where(first, p0 / total, jnp.where(second, p1 / total, 0.0))
            rank = jnp.dot(named.astype(BF16), earlier, preferred_element_type=F32)
            slot = jnp.where(named > 0.5, rank, -1.0)
            weighted = []
            for k in range(nh):
                chosen = jnp.where(slot_id == slot[k:k + 1, :], 1.0, 0.0)
                pick[st, p, pl.ds(k * slots, slots), :] = chosen.astype(BF16)
                weighted.append(chosen * gate[k:k + 1, :])
            flat = jnp.concatenate(weighted, axis=0).T
            top = flat.astype(BF16)
            comb[st, p, 0] = top
            comb[st, p, 1] = (flat - top.astype(F32)).astype(BF16)

    def own(st, c):
        relay(st, c).wait_recv()
        to_proxy(st, c, my_q).start()
        rows = jnp.dot(pick[st, 0], arrived[st, c], preferred_element_type=F32).astype(BF16)
        received[st, 0, c, 0] = rows[:slots]
        for k in range(1, nh):
            out_own[st, c, k] = rows[k * slots:(k + 1) * slots]
            send_own(st, c, k).start()

    def proxied(st, c):
        for q in range(2):
            to_proxy(st, c, q).wait_recv()
            rows = jnp.dot(pick[st, 1 + q], raw[st, q, c], preferred_element_type=F32).astype(BF16)
            received[st, 1, c, 2 * pos + q] = rows[:slots]
            for k in range(1, nh):
                if st == 1:
                    send_proxied(0, q, c, k, 2 * pos + q).wait_send()
                out_proxy[q, c, k] = rows[k * slots:(k + 1) * slots]
                send_proxied(st, q, c, k, 2 * pos + q).start()

    def experts(st, g):
        acc_g[...] = jnp.zeros_like(acc_g)
        acc_u[...] = jnp.zeros_like(acc_u)

        @pl.loop(0, nh)
        def _(c):
            if g == 0:
                for k in range(1, nh):
                    send_own(st, c, k).wait_recv()
            else:
                for j in range(nq):
                    @pl.when(jnp.logical_not(mid & (pos == j)))
                    def _():
                        for q in range(2):
                            send_proxied(st, q, c, 1, 2 * j + q).wait_recv()

            x = received[st, g, c].reshape(nh * slots, width)
            acc_g[...] += jnp.dot(x, wg[columns(c), :], preferred_element_type=F32)
            acc_u[...] += jnp.dot(x, wu[columns(c), :], preferred_element_type=F32)

        gate = acc_g[...]
        hidden[...] = (gate / (1.0 + jnp.exp(-gate)) * acc_u[...]).astype(BF16)

        @pl.loop(0, nh)
        def _(c):
            y = jnp.dot(hidden[...], wd[:, columns(c)], preferred_element_type=F32).astype(BF16)
            if g == 0:
                returned[st, 0, c, 0] = y[:slots]
                for k in range(1, nh):
                    received[st, 0, c, k] = y[k * slots:(k + 1) * slots]
                    return_own(st, c, k).start()
            else:
                for j in range(nq):
                    blocks = [y[(2 * j + q) * slots:(2 * j + q + 1) * slots] for q in range(2)]
                    myself = mid & (pos == j)

                    @pl.when(myself)
                    def _():
                        for q in range(2):
                            returned[st, 1 + q, c, 0] = blocks[q]

                    @pl.when(jnp.logical_not(myself))
                    def _():
                        offset = lax.rem(loc - first_mid - j + nh, nh)
                        for q in range(2):
                            received[st, 1, c, 2 * j + q] = blocks[q]
                            return_proxied(st, q, c, j, offset).start()

    def weighted_sum(st, p, c):
        rows = returned[st, p, c].reshape(nh * slots, width)
        return (jnp.dot(comb[st, p, 0], rows, preferred_element_type=F32)
                + jnp.dot(comb[st, p, 1], rows, preferred_element_type=F32))

    def proxy_sum(st, c):
        for q in range(2):
            for k in range(1, nh):
                return_proxied(st, q, c, 0, k).wait_recv()
            raw[st, q, c] = weighted_sum(st, 1 + q, c).astype(BF16)
            from_proxy(st, q, c).start()

    def finish(st, c):
        for k in range(1, nh):
            return_own(st, c, k).wait_recv()
        total = arrived[st, c].astype(F32) + weighted_sum(st, 0, c)
        from_proxy(st, 0, c).wait_recv()
        outs[st][0, :, columns(c)] = (total + part[st, c].astype(F32)).astype(BF16)

    tables(meta_here[...], 0)

    @pl.loop(0, nh)
    def _(c):
        own(0, c)
        relay(1, c).start()

    @pl.when(mid)
    def _():
        for q in range(2):
            meta_copy(q).wait_recv()
            tables(meta_there[q], 1 + q)

        @pl.loop(0, nh)
        def _(c):
            proxied(0, c)
            own(1, c)

    @pl.when(jnp.logical_not(mid))
    def _():
        @pl.loop(0, nh)
        def _(c):
            own(1, c)

    for i in range(3):
        local_copies[i].wait()
        core_copies[i].wait_recv()

    experts(0, 0)
    experts(0, 1)

    @pl.when(mid)
    def _():
        @pl.loop(0, nh)
        def _(c):
            proxied(1, c)

    experts(1, 0)

    @pl.when(mid)
    def _():
        @pl.loop(0, nh)
        def _(c):
            proxy_sum(0, c)

    experts(1, 1)

    @pl.when(mid)
    def _():
        @pl.loop(0, nh)
        def _(c):
            proxy_sum(1, c)

    @pl.loop(0, nh)
    def _(c):
        finish(0, c)

    @pl.loop(0, nh)
    def _(c):
        finish(1, c)

    meta_copy(my_q).wait_send()
    for i in range(3):
        core_copies[i].wait_send()

    @pl.loop(0, nh)
    def _(c):
        for st in range(2):
            relay(st, c).wait_send()
            to_proxy(st, c, my_q).wait_send()
            for k in range(1, nh):
                send_own(st, c, k).wait_send()
                return_own(st, c, k).wait_send()
            for j in range(nq):
                @pl.when(jnp.logical_not(mid & (pos == j)))
                def _():
                    for q in range(2):
                        return_proxied(st, q, c, j, 1).wait_send()

    @pl.when(mid)
    def _():
        @pl.loop(0, nh)
        def _(c):
            for q in range(2):
                for st in range(2):
                    from_proxy(st, q, c).wait_send()
                for k in range(1, nh):
                    send_proxied(1, q, c, k, 2 * pos + q).wait_send()


def body(act_fwd, act_rev, ids_fwd, ids_rev, probs_fwd, probs_rev, w_gate, w_up, w_down):
    tokens, top = ids_fwd.shape[1:]
    model = act_fwd.shape[2]
    units = w_gate.shape[2]
    experts = lax.axis_size("expert") // 2
    nh = experts // 2
    width = model // nh
    cap = 2 * (3 * tokens * top // (4 * experts))
    slots = -(-cap // 16) * 16
    meta = jnp.concatenate(
        [ids_fwd[0].astype(F32), ids_rev[0].astype(F32), probs_fwd[0], probs_rev[0]], axis=1
    ).T
    anywhere = pl.BlockSpec(memory_space=pl.ANY)
    vmem = pl.BlockSpec(memory_space=pltpu.VMEM)
    dma = pltpu.SemaphoreType.DMA
    out = jax.ShapeDtypeStruct((1, tokens, model), BF16)
    return pl.pallas_call(
        functools.partial(kernel, lax.axis_size("section"), nh, slots, width),
        out_shape=(out, out),
        in_specs=[anywhere, anywhere, vmem, anywhere, anywhere, anywhere],
        out_specs=(vmem, vmem),
        scratch_shapes=[
            pltpu.VMEM((model, 2 * units), BF16),
            pltpu.VMEM((model, 2 * units), BF16),
            pltpu.VMEM((2 * units, model), BF16),
            pltpu.VMEM((2, 8, tokens), F32),
            pltpu.VMEM((2, nh, tokens, width), BF16),
            pltpu.VMEM((2, 2, nh, tokens, width), BF16),
            pltpu.VMEM((2, nh, nh, slots, width), BF16),
            pltpu.VMEM((2, nh, nh, slots, width), BF16),
            pltpu.VMEM((2, 2, nh, nh, slots, width), BF16),
            pltpu.VMEM((2, 3, nh, nh, slots, width), BF16),
            pltpu.VMEM((2, nh, tokens, width), BF16),
            pltpu.VMEM((2, 3, nh * slots, tokens), BF16),
            pltpu.VMEM((2, 3, 2, tokens, nh * slots), BF16),
            pltpu.VMEM((nh * slots, 2 * units), F32),
            pltpu.VMEM((nh * slots, 2 * units), F32),
            pltpu.VMEM((nh * slots, 2 * units), BF16),
            dma((3,)), dma((3,)), dma((3,)), dma, dma((2,)),
            dma((2, nh)), dma((2, nh)), dma((2, nh)), dma((2, 2, nh)),
            dma((2, 3, nh, nh)), dma((2, 2, nh, nh)), dma((2, 2, nh, nh)), dma((2, 3, nh, nh)),
            dma((2, 2, nh)), dma((2, nh)),
        ],
        compiler_params=pltpu.CompilerParams(
            collective_id=0, has_side_effects=True, vmem_limit_bytes=63 * 1024 * 1024
        ),
        cost_estimate=pl.CostEstimate(
            flops=12 * experts * cap * model * 2 * units,
            bytes_accessed=12 * model * units + 8 * tokens * model,
            transcendentals=0,
        ),
    )(act_fwd, act_rev, meta, w_gate, w_up, w_down)


def solution(mesh):
    return jax.shard_map(
        body,
        mesh=mesh,
        in_specs=(
            P("section", "expert", None),
            P("section", "expert", None),
            P("section", "expert", None),
            P("section", "expert", None),
            P("section", "expert", None),
            P("section", "expert", None),
            P("section", None, "expert"),
            P("section", None, "expert"),
            P("section", "expert", None),
        ),
        out_specs=(P("section", "expert", None), P("section", "expert", None)),
        check_vma=False,
    )
```

```python
import functools

import jax
import jax.numpy as jnp
from jax import lax
from jax.experimental import pallas as pl
from jax.experimental.pallas import tpu as pltpu
from jax.sharding import PartitionSpec as P

MESH = pl.DeviceIdType.MESH
F32 = jnp.float32
BF16 = jnp.bfloat16


def kernel(
    sections, nh, slots, width,
    act_f, act_r, meta_here, w_gate, w_up, w_down,
    out_f, out_r,
    wg, wu, wd, meta_there, arrived, raw, out_own, out_proxy, received, returned, part, pick, comb,
    acc_g, acc_u, hidden,
    w_local, w_send, w_recv, meta_send, meta_recv, relay_send, relay_recv, raw_send, raw_recv,
    disp_send, disp_recv, ret_send, ret_recv, part_send, part_recv,
):
    half_units = w_gate.shape[-1]
    tokens = arrived.shape[2]
    nq = nh // 2
    section = lax.axis_index("section")
    me = lax.axis_index("expert")
    core = lax.rem(me, 2)
    chip = me // 2
    half = chip // nh
    loc = lax.rem(chip, nh)
    pos = lax.rem(loc, nq)
    mid = (loc // nq) == (1 - half)
    my_q = jnp.where(mid, 0, 1)
    first_mid = nq * (1 - half)

    def at_chip(c):
        return (section, c * 2 + core)

    def in_half(offset):
        return at_chip(half * nh + lax.rem(loc + offset + nh, nh))

    def mid_peer(j):
        return at_chip(half * nh + first_mid + j)

    proxy = at_chip((1 - half) * nh + nq * half + pos)
    sources = (proxy, at_chip((1 - half) * nh + nq * (1 - half) + pos))
    other_core = (section, chip * 2 + 1 - core)
    after = (lax.rem(section + 1, sections), me)
    before = (lax.rem(section + sections - 1, sections), me)
    acts, outs, ways = (act_f, act_r), (out_f, out_r), (after, before)

    def columns(c):
        return pl.ds(pl.multiple_of(c * width, width), width)

    def remote(src, dst, send, recv, device):
        return pltpu.make_async_remote_copy(
            src_ref=src, dst_ref=dst, send_sem=send, recv_sem=recv,
            device_id=device, device_id_type=MESH,
        )

    def relay(st, c):
        return remote(acts[st].at[0, :, columns(c)], arrived.at[st, c],
                      relay_send.at[st, c], relay_recv.at[st, c], ways[st])

    def to_proxy(st, c, q):
        return remote(arrived.at[st, c], raw.at[st, q, c],
                      raw_send.at[st, c], raw_recv.at[st, q, c], proxy)

    def send_own(st, c, k):
        return remote(out_own.at[st, c, k], received.at[st, 0, c, k],
                      disp_send.at[st, 0, c, k], disp_recv.at[st, 0, c, k], in_half(k))

    def send_proxied(st, q, c, k, block):
        return remote(out_proxy.at[q, c, k], received.at[st, 1, c, block],
                      disp_send.at[st, 1 + q, c, k], disp_recv.at[st, 1, c, block], in_half(k))

    def return_own(st, c, k):
        return remote(received.at[st, 0, c, k], returned.at[st, 0, c, k],
                      ret_send.at[st, 0, c, k], ret_recv.at[st, 0, c, k], in_half(-k))

    def return_proxied(st, q, c, j, k):
        block = 2 * j + q
        return remote(received.at[st, 1, c, block], returned.at[st, 1 + q, c, k],
                      ret_send.at[st, 1, c, block], ret_recv.at[st, 1 + q, c, k], mid_peer(j))

    def from_proxy(st, q, c):
        return remote(raw.at[st, q, c], part.at[st, c],
                      part_send.at[st, q, c], part_recv.at[st, c], sources[q])

    def meta_copy(q):
        return remote(meta_here, meta_there.at[q], meta_send, meta_recv.at[q], proxy)

    barrier = pltpu.get_barrier_semaphore()
    greeted = [after, before, proxy, other_core] + [in_half(k) for k in range(1, nh)]
    for device in greeted:
        pl.semaphore_signal(barrier, inc=1, device_id=device, device_id_type=MESH)

    @pl.when(mid)
    def _():
        for device in sources:
            pl.semaphore_signal(barrier, inc=1, device_id=device, device_id_type=MESH)

    pl.semaphore_wait(barrier, len(greeted) + jnp.where(mid, 2, 0))

    @pl.loop(0, nh)
    def _(c):
        relay(0, c).start()

    meta_copy(my_q).start()

    here, there = pl.ds(0, half_units), pl.ds(half_units, half_units)
    places = ((w_gate, wg.at[:, here], wg.at[:, there]), (w_up, wu.at[:, here], wu.at[:, there]),
              (w_down, wd.at[here, :], wd.at[there, :]))
    local_copies, core_copies = [], []
    for i, (w, mine, theirs) in enumerate(places):
        local_copies.append(pltpu.make_async_copy(w.at[0], mine, w_local.at[i]))
        core_copies.append(remote(w.at[0], theirs, w_send.at[i], w_recv.at[i], other_core))
        local_copies[i].start()
        core_copies[i].start()

    row = lax.broadcasted_iota(jnp.int32, (tokens, tokens), 0)
    col = lax.broadcasted_iota(jnp.int32, (tokens, tokens), 1)
    earlier = jnp.where(row < col, 1.0, 0.0).astype(BF16)
    turn = loc + lax.broadcasted_iota(jnp.int32, (8, tokens), 0)
    expert = (half * nh + jnp.where(turn >= nh, turn - nh, turn)).astype(F32)
    slot_id = lax.broadcasted_iota(jnp.int32, (slots, tokens), 0).astype(F32)

    def tables(meta, p):
        for st in range(2):
            i0, i1 = meta[2 * st:2 * st + 1, :], meta[2 * st + 1:2 * st + 2, :]
            p0, p1 = meta[4 + 2 * st:5 + 2 * st, :], meta[5 + 2 * st:6 + 2 * st, :]
            total = p0 + p1
            first, second = i0 == expert, i1 == expert
            named = jnp.where(first, 1.0, jnp.where(second, 1.0, 0.0))
            gate = jnp.where(first, p0 / total, jnp.where(second, p1 / total, 0.0))
            rank = jnp.dot(named.astype(BF16), earlier, preferred_element_type=F32)
            slot = jnp.where(named > 0.5, rank, -1.0)
            weighted = []
            for k in range(nh):
                chosen = jnp.where(slot_id == slot[k:k + 1, :], 1.0, 0.0)
                pick[st, p, pl.ds(k * slots, slots), :] = chosen.astype(BF16)
                weighted.append(chosen * gate[k:k + 1, :])
            flat = jnp.concatenate(weighted, axis=0).T
            top = flat.astype(BF16)
            comb[st, p, 0] = top
            comb[st, p, 1] = (flat - top.astype(F32)).astype(BF16)

    def own(st, c):
        relay(st, c).wait_recv()
        to_proxy(st, c, my_q).start()
        rows = jnp.dot(pick[st, 0], arrived[st, c], preferred_element_type=F32).astype(BF16)
        received[st, 0, c, 0] = rows[:slots]
        for k in range(1, nh):
            out_own[st, c, k] = rows[k * slots:(k + 1) * slots]
            send_own(st, c, k).start()

    def proxied(st, c):
        for q in range(2):
            to_proxy(st, c, q).wait_recv()
            rows = jnp.dot(pick[st, 1 + q], raw[st, q, c], preferred_element_type=F32).astype(BF16)
            received[st, 1, c, 2 * pos + q] = rows[:slots]
            for k in range(1, nh):
                if st == 1:
                    send_proxied(0, q, c, k, 2 * pos + q).wait_send()
                out_proxy[q, c, k] = rows[k * slots:(k + 1) * slots]
                send_proxied(st, q, c, k, 2 * pos + q).start()

    def experts(st, g):
        acc_g[...] = jnp.zeros_like(acc_g)
        acc_u[...] = jnp.zeros_like(acc_u)

        @pl.loop(0, nh)
        def _(c):
            if g == 0:
                for k in range(1, nh):
                    send_own(st, c, k).wait_recv()
            else:
                for j in range(nq):
                    @pl.when(jnp.logical_not(mid & (pos == j)))
                    def _():
                        for q in range(2):
                            send_proxied(st, q, c, 1, 2 * j + q).wait_recv()

            x = received[st, g, c].reshape(nh * slots, width)
            acc_g[...] += jnp.dot(x, wg[columns(c), :], preferred_element_type=F32)
            acc_u[...] += jnp.dot(x, wu[columns(c), :], preferred_element_type=F32)

        gate = acc_g[...]
        hidden[...] = (gate / (1.0 + jnp.exp(-gate)) * acc_u[...]).astype(BF16)

        @pl.loop(0, nh)
        def _(c):
            y = jnp.dot(hidden[...], wd[:, columns(c)], preferred_element_type=F32).astype(BF16)
            if g == 0:
                returned[st, 0, c, 0] = y[:slots]
                for k in range(1, nh):
                    received[st, 0, c, k] = y[k * slots:(k + 1) * slots]
                    return_own(st, c, k).start()
            else:
                for j in range(nq):
                    blocks = [y[(2 * j + q) * slots:(2 * j + q + 1) * slots] for q in range(2)]
                    myself = mid & (pos == j)

                    @pl.when(myself)
                    def _():
                        for q in range(2):
                            returned[st, 1 + q, c, 0] = blocks[q]

                    @pl.when(jnp.logical_not(myself))
                    def _():
                        offset = lax.rem(loc - first_mid - j + nh, nh)
                        for q in range(2):
                            received[st, 1, c, 2 * j + q] = blocks[q]
                            return_proxied(st, q, c, j, offset).start()

    def weighted_sum(st, p, c):
        rows = returned[st, p, c].reshape(nh * slots, width)
        return (jnp.dot(comb[st, p, 0], rows, preferred_element_type=F32)
                + jnp.dot(comb[st, p, 1], rows, preferred_element_type=F32))

    def proxy_sum(st, c):
        for q in range(2):
            for k in range(1, nh):
                return_proxied(st, q, c, 0, k).wait_recv()
            raw[st, q, c] = weighted_sum(st, 1 + q, c).astype(BF16)
            from_proxy(st, q, c).start()

    def finish(st, c):
        for k in range(1, nh):
            return_own(st, c, k).wait_recv()
        total = arrived[st, c].astype(F32) + weighted_sum(st, 0, c)
        from_proxy(st, 0, c).wait_recv()
        outs[st][0, :, columns(c)] = (total + part[st, c].astype(F32)).astype(BF16)

    tables(meta_here[...], 0)

    @pl.loop(0, nh)
    def _(c):
        own(0, c)
        relay(1, c).start()

    @pl.when(mid)
    def _():
        for q in range(2):
            meta_copy(q).wait_recv()
            tables(meta_there[q], 1 + q)

        @pl.loop(0, nh)
        def _(c):
            proxied(0, c)
            own(1, c)

    @pl.when(jnp.logical_not(mid))
    def _():
        @pl.loop(0, nh)
        def _(c):
            own(1, c)

    for i in range(3):
        local_copies[i].wait()
        core_copies[i].wait_recv()

    experts(0, 0)
    experts(1, 0)

    @pl.when(mid)
    def _():
        proxied(1, 0)

    experts(0, 1)

    @pl.when(mid)
    def _():
        @pl.loop(1, nh)
        def _(c):
            proxied(1, c)

        @pl.loop(0, nq)
        def _(c):
            proxy_sum(0, c)

    experts(1, 1)

    @pl.when(mid)
    def _():
        @pl.loop(nq, nh)
        def _(c):
            proxy_sum(0, c)

    @pl.when(mid)
    def _():
        @pl.loop(0, nh)
        def _(c):
            proxy_sum(1, c)

    @pl.loop(0, nh)
    def _(c):
        finish(0, c)

    @pl.loop(0, nh)
    def _(c):
        finish(1, c)

    meta_copy(my_q).wait_send()
    for i in range(3):
        core_copies[i].wait_send()

    @pl.loop(0, nh)
    def _(c):
        for st in range(2):
            relay(st, c).wait_send()
            to_proxy(st, c, my_q).wait_send()
            for k in range(1, nh):
                send_own(st, c, k).wait_send()
                return_own(st, c, k).wait_send()
            for j in range(nq):
                @pl.when(jnp.logical_not(mid & (pos == j)))
                def _():
                    for q in range(2):
                        return_proxied(st, q, c, j, 1).wait_send()

    @pl.when(mid)
    def _():
        @pl.loop(0, nh)
        def _(c):
            for q in range(2):
                for st in range(2):
                    from_proxy(st, q, c).wait_send()
                for k in range(1, nh):
                    send_proxied(1, q, c, k, 2 * pos + q).wait_send()


def body(act_fwd, act_rev, ids_fwd, ids_rev, probs_fwd, probs_rev, w_gate, w_up, w_down):
    tokens, top = ids_fwd.shape[1:]
    model = act_fwd.shape[2]
    units = w_gate.shape[2]
    experts = lax.axis_size("expert") // 2
    nh = experts // 2
    width = model // nh
    cap = 2 * (3 * tokens * top // (4 * experts))
    slots = -(-cap // 16) * 16
    meta = jnp.concatenate(
        [ids_fwd[0].astype(F32), ids_rev[0].astype(F32), probs_fwd[0], probs_rev[0]], axis=1
    ).T
    anywhere = pl.BlockSpec(memory_space=pl.ANY)
    vmem = pl.BlockSpec(memory_space=pltpu.VMEM)
    dma = pltpu.SemaphoreType.DMA
    out = jax.ShapeDtypeStruct((1, tokens, model), BF16)
    return pl.pallas_call(
        functools.partial(kernel, lax.axis_size("section"), nh, slots, width),
        out_shape=(out, out),
        in_specs=[anywhere, anywhere, vmem, anywhere, anywhere, anywhere],
        out_specs=(vmem, vmem),
        scratch_shapes=[
            pltpu.VMEM((model, 2 * units), BF16),
            pltpu.VMEM((model, 2 * units), BF16),
            pltpu.VMEM((2 * units, model), BF16),
            pltpu.VMEM((2, 8, tokens), F32),
            pltpu.VMEM((2, nh, tokens, width), BF16),
            pltpu.VMEM((2, 2, nh, tokens, width), BF16),
            pltpu.VMEM((2, nh, nh, slots, width), BF16),
            pltpu.VMEM((2, nh, nh, slots, width), BF16),
            pltpu.VMEM((2, 2, nh, nh, slots, width), BF16),
            pltpu.VMEM((2, 3, nh, nh, slots, width), BF16),
            pltpu.VMEM((2, nh, tokens, width), BF16),
            pltpu.VMEM((2, 3, nh * slots, tokens), BF16),
            pltpu.VMEM((2, 3, 2, tokens, nh * slots), BF16),
            pltpu.VMEM((nh * slots, 2 * units), F32),
            pltpu.VMEM((nh * slots, 2 * units), F32),
            pltpu.VMEM((nh * slots, 2 * units), BF16),
            dma((3,)), dma((3,)), dma((3,)), dma, dma((2,)),
            dma((2, nh)), dma((2, nh)), dma((2, nh)), dma((2, 2, nh)),
            dma((2, 3, nh, nh)), dma((2, 2, nh, nh)), dma((2, 2, nh, nh)), dma((2, 3, nh, nh)),
            dma((2, 2, nh)), dma((2, nh)),
        ],
        compiler_params=pltpu.CompilerParams(
            collective_id=0, has_side_effects=True, vmem_limit_bytes=63 * 1024 * 1024
        ),
        cost_estimate=pl.CostEstimate(
            flops=12 * experts * cap * model * 2 * units,
            bytes_accessed=12 * model * units + 8 * tokens * model,
            transcendentals=0,
        ),
    )(act_fwd, act_rev, meta, w_gate, w_up, w_down)


def solution(mesh):
    return jax.shard_map(
        body,
        mesh=mesh,
        in_specs=(
            P("section", "expert", None),
            P("section", "expert", None),
            P("section", "expert", None),
            P("section", "expert", None),
            P("section", "expert", None),
            P("section", "expert", None),
            P("section", None, "expert"),
            P("section", None, "expert"),
            P("section", "expert", None),
        ),
        out_specs=(P("section", "expert", None), P("section", "expert", None)),
        check_vma=False,
    )
```

```python
import functools

import jax
import jax.numpy as jnp
from jax import lax
from jax.experimental import pallas as pl
from jax.experimental.pallas import tpu as pltpu
from jax.sharding import PartitionSpec as P

MESH = pl.DeviceIdType.MESH
F32 = jnp.float32
BF16 = jnp.bfloat16


def kernel(
    sections, nh, slots, width,
    act_f, act_r, meta_here, w_gate, w_up, w_down,
    out_f, out_r,
    wg, wu, wd, meta_there, arrived, raw, out_own, out_proxy, received, returned, part, pick, comb,
    acc_g, acc_u, hidden,
    w_local, w_send, w_recv, meta_send, meta_recv, relay_send, relay_recv, raw_send, raw_recv,
    disp_send, disp_recv, ret_send, ret_recv, part_send, part_recv,
):
    half_units = w_gate.shape[-1]
    tokens = arrived.shape[2]
    nq = nh // 2
    section = lax.axis_index("section")
    me = lax.axis_index("expert")
    core = lax.rem(me, 2)
    chip = me // 2
    half = chip // nh
    loc = lax.rem(chip, nh)
    pos = lax.rem(loc, nq)
    mid = (loc // nq) == (1 - half)
    my_q = jnp.where(mid, 0, 1)
    first_mid = nq * (1 - half)

    def at_chip(c):
        return (section, c * 2 + core)

    def in_half(offset):
        return at_chip(half * nh + lax.rem(loc + offset + nh, nh))

    def mid_peer(j):
        return at_chip(half * nh + first_mid + j)

    proxy = at_chip((1 - half) * nh + nq * half + pos)
    sources = (proxy, at_chip((1 - half) * nh + nq * (1 - half) + pos))
    other_core = (section, chip * 2 + 1 - core)
    after = (lax.rem(section + 1, sections), me)
    before = (lax.rem(section + sections - 1, sections), me)
    acts, outs, ways = (act_f, act_r), (out_f, out_r), (after, before)

    def columns(c):
        return pl.ds(pl.multiple_of(c * width, width), width)

    def remote(src, dst, send, recv, device):
        return pltpu.make_async_remote_copy(
            src_ref=src, dst_ref=dst, send_sem=send, recv_sem=recv,
            device_id=device, device_id_type=MESH,
        )

    def relay(st, c):
        return remote(acts[st].at[0, :, columns(c)], arrived.at[st, c],
                      relay_send.at[st, c], relay_recv.at[st, c], ways[st])

    def to_proxy(st, c, q):
        return remote(arrived.at[st, c], raw.at[st, q, c],
                      raw_send.at[st, c], raw_recv.at[st, q, c], proxy)

    def send_own(st, c, k):
        return remote(out_own.at[st, c, k], received.at[st, 0, c, k],
                      disp_send.at[st, 0, c, k], disp_recv.at[st, 0, c, k], in_half(k))

    def send_proxied(st, q, c, k, block):
        return remote(out_proxy.at[q, c, k], received.at[st, 1, c, block],
                      disp_send.at[st, 1 + q, c, k], disp_recv.at[st, 1, c, block], in_half(k))

    def return_own(st, c, k):
        return remote(received.at[st, 0, c, k], returned.at[st, 0, c, k],
                      ret_send.at[st, 0, c, k], ret_recv.at[st, 0, c, k], in_half(-k))

    def return_proxied(st, q, c, j, k):
        block = 2 * j + q
        return remote(received.at[st, 1, c, block], returned.at[st, 1 + q, c, k],
                      ret_send.at[st, 1, c, block], ret_recv.at[st, 1 + q, c, k], mid_peer(j))

    def from_proxy(st, q, c):
        return remote(raw.at[st, q, c], part.at[st, c],
                      part_send.at[st, q, c], part_recv.at[st, c], sources[q])

    def meta_copy(q):
        return remote(meta_here, meta_there.at[q], meta_send, meta_recv.at[q], proxy)

    barrier = pltpu.get_barrier_semaphore()
    greeted = [after, before, proxy, other_core] + [in_half(k) for k in range(1, nh)]
    for device in greeted:
        pl.semaphore_signal(barrier, inc=1, device_id=device, device_id_type=MESH)

    @pl.when(mid)
    def _():
        for device in sources:
            pl.semaphore_signal(barrier, inc=1, device_id=device, device_id_type=MESH)

    pl.semaphore_wait(barrier, len(greeted) + jnp.where(mid, 2, 0))

    @pl.loop(0, nh)
    def _(c):
        relay(0, c).start()

    meta_copy(my_q).start()

    here, there = pl.ds(0, half_units), pl.ds(half_units, half_units)
    places = ((w_gate, wg.at[:, here], wg.at[:, there]), (w_up, wu.at[:, here], wu.at[:, there]),
              (w_down, wd.at[here, :], wd.at[there, :]))
    local_copies, core_copies = [], []
    for i, (w, mine, theirs) in enumerate(places):
        local_copies.append(pltpu.make_async_copy(w.at[0], mine, w_local.at[i]))
        core_copies.append(remote(w.at[0], theirs, w_send.at[i], w_recv.at[i], other_core))
        local_copies[i].start()
        core_copies[i].start()

    row = lax.broadcasted_iota(jnp.int32, (tokens, tokens), 0)
    col = lax.broadcasted_iota(jnp.int32, (tokens, tokens), 1)
    earlier = jnp.where(row < col, 1.0, 0.0).astype(BF16)
    turn = loc + lax.broadcasted_iota(jnp.int32, (8, tokens), 0)
    expert = (half * nh + jnp.where(turn >= nh, turn - nh, turn)).astype(F32)
    slot_id = lax.broadcasted_iota(jnp.int32, (slots, tokens), 0).astype(F32)

    def tables(meta, p):
        for st in range(2):
            i0, i1 = meta[2 * st:2 * st + 1, :], meta[2 * st + 1:2 * st + 2, :]
            p0, p1 = meta[4 + 2 * st:5 + 2 * st, :], meta[5 + 2 * st:6 + 2 * st, :]
            total = p0 + p1
            first, second = i0 == expert, i1 == expert
            named = jnp.where(first, 1.0, jnp.where(second, 1.0, 0.0))
            gate = jnp.where(first, p0 / total, jnp.where(second, p1 / total, 0.0))
            rank = jnp.dot(named.astype(BF16), earlier, preferred_element_type=F32)
            slot = jnp.where(named > 0.5, rank, -1.0)
            weighted = []
            for k in range(nh):
                chosen = jnp.where(slot_id == slot[k:k + 1, :], 1.0, 0.0)
                pick[st, p, pl.ds(k * slots, slots), :] = chosen.astype(BF16)
                weighted.append(chosen * gate[k:k + 1, :])
            flat = jnp.concatenate(weighted, axis=0).T
            top = flat.astype(BF16)
            comb[st, p, 0] = top
            comb[st, p, 1] = (flat - top.astype(F32)).astype(BF16)

    def own(st, c):
        relay(st, c).wait_recv()
        to_proxy(st, c, my_q).start()
        rows = jnp.dot(pick[st, 0], arrived[st, c], preferred_element_type=F32).astype(BF16)
        received[st, 0, c, 0] = rows[:slots]
        for k in range(1, nh):
            out_own[st, c, k] = rows[k * slots:(k + 1) * slots]
            send_own(st, c, k).start()

    def proxied(st, c):
        for q in range(2):
            to_proxy(st, c, q).wait_recv()
            rows = jnp.dot(pick[st, 1 + q], raw[st, q, c], preferred_element_type=F32).astype(BF16)
            received[st, 1, c, 2 * pos + q] = rows[:slots]
            for k in range(1, nh):
                if st == 1:
                    send_proxied(0, q, c, k, 2 * pos + q).wait_send()
                out_proxy[q, c, k] = rows[k * slots:(k + 1) * slots]
                send_proxied(st, q, c, k, 2 * pos + q).start()

    def experts(st, g):
        acc_g[...] = jnp.zeros_like(acc_g)
        acc_u[...] = jnp.zeros_like(acc_u)

        @pl.loop(0, nh)
        def _(c):
            if g == 0:
                for k in range(1, nh):
                    send_own(st, c, k).wait_recv()
            else:
                for j in range(nq):
                    @pl.when(jnp.logical_not(mid & (pos == j)))
                    def _():
                        for q in range(2):
                            send_proxied(st, q, c, 1, 2 * j + q).wait_recv()

            x = received[st, g, c].reshape(nh * slots, width)
            acc_g[...] += jnp.dot(x, wg[columns(c), :], preferred_element_type=F32)
            acc_u[...] += jnp.dot(x, wu[columns(c), :], preferred_element_type=F32)

        gate = acc_g[...]
        hidden[...] = (gate / (1.0 + jnp.exp(-gate)) * acc_u[...]).astype(BF16)

        @pl.loop(0, nh)
        def _(c):
            y = jnp.dot(hidden[...], wd[:, columns(c)], preferred_element_type=F32).astype(BF16)
            if g == 0:
                returned[st, 0, c, 0] = y[:slots]
                for k in range(1, nh):
                    received[st, 0, c, k] = y[k * slots:(k + 1) * slots]
                    return_own(st, c, k).start()
            else:
                for j in range(nq):
                    blocks = [y[(2 * j + q) * slots:(2 * j + q + 1) * slots] for q in range(2)]
                    myself = mid & (pos == j)

                    @pl.when(myself)
                    def _():
                        for q in range(2):
                            returned[st, 1 + q, c, 0] = blocks[q]

                    @pl.when(jnp.logical_not(myself))
                    def _():
                        offset = lax.rem(loc - first_mid - j + nh, nh)
                        for q in range(2):
                            received[st, 1, c, 2 * j + q] = blocks[q]
                            return_proxied(st, q, c, j, offset).start()

    def weighted_sum(st, p, c):
        rows = returned[st, p, c].reshape(nh * slots, width)
        return (jnp.dot(comb[st, p, 0], rows, preferred_element_type=F32)
                + jnp.dot(comb[st, p, 1], rows, preferred_element_type=F32))

    def proxy_sum(st, c):
        for q in range(2):
            for k in range(1, nh):
                return_proxied(st, q, c, 0, k).wait_recv()
            raw[st, q, c] = weighted_sum(st, 1 + q, c).astype(BF16)
            from_proxy(st, q, c).start()

    def finish(st, c):
        for k in range(1, nh):
            return_own(st, c, k).wait_recv()
        total = arrived[st, c].astype(F32) + weighted_sum(st, 0, c)
        from_proxy(st, 0, c).wait_recv()
        outs[st][0, :, columns(c)] = (total + part[st, c].astype(F32)).astype(BF16)

    tables(meta_here[...], 0)

    @pl.loop(0, nh)
    def _(c):
        own(0, c)
        relay(1, c).start()

    @pl.when(mid)
    def _():
        for q in range(2):
            meta_copy(q).wait_recv()
            tables(meta_there[q], 1 + q)

        @pl.loop(0, nh)
        def _(c):
            proxied(0, c)

        @pl.loop(0, nh)
        def _(c):
            own(1, c)

    for i in range(3):
        local_copies[i].wait()
        core_copies[i].wait_recv()

    experts(0, 0)

    @pl.when(jnp.logical_not(mid))
    def _():
        @pl.loop(0, nh)
        def _(c):
            own(1, c)

    experts(0, 1)

    @pl.when(mid)
    def _():
        @pl.loop(0, nh)
        def _(c):
            proxied(1, c)

    experts(1, 0)

    @pl.when(mid)
    def _():
        @pl.loop(0, nh)
        def _(c):
            proxy_sum(0, c)

    experts(1, 1)

    @pl.when(mid)
    def _():
        @pl.loop(0, nh)
        def _(c):
            proxy_sum(1, c)

    @pl.loop(0, nh)
    def _(c):
        finish(0, c)

    @pl.loop(0, nh)
    def _(c):
        finish(1, c)

    meta_copy(my_q).wait_send()
    for i in range(3):
        core_copies[i].wait_send()

    @pl.loop(0, nh)
    def _(c):
        for st in range(2):
            relay(st, c).wait_send()
            to_proxy(st, c, my_q).wait_send()
            for k in range(1, nh):
                send_own(st, c, k).wait_send()
                return_own(st, c, k).wait_send()
            for j in range(nq):
                @pl.when(jnp.logical_not(mid & (pos == j)))
                def _():
                    for q in range(2):
                        return_proxied(st, q, c, j, 1).wait_send()

    @pl.when(mid)
    def _():
        @pl.loop(0, nh)
        def _(c):
            for q in range(2):
                for st in range(2):
                    from_proxy(st, q, c).wait_send()
                for k in range(1, nh):
                    send_proxied(1, q, c, k, 2 * pos + q).wait_send()


def body(act_fwd, act_rev, ids_fwd, ids_rev, probs_fwd, probs_rev, w_gate, w_up, w_down):
    tokens, top = ids_fwd.shape[1:]
    model = act_fwd.shape[2]
    units = w_gate.shape[2]
    experts = lax.axis_size("expert") // 2
    nh = experts // 2
    width = model // nh
    cap = 2 * (3 * tokens * top // (4 * experts))
    slots = -(-cap // 16) * 16
    meta = jnp.concatenate(
        [ids_fwd[0].astype(F32), ids_rev[0].astype(F32), probs_fwd[0], probs_rev[0]], axis=1
    ).T
    anywhere = pl.BlockSpec(memory_space=pl.ANY)
    vmem = pl.BlockSpec(memory_space=pltpu.VMEM)
    dma = pltpu.SemaphoreType.DMA
    out = jax.ShapeDtypeStruct((1, tokens, model), BF16)
    return pl.pallas_call(
        functools.partial(kernel, lax.axis_size("section"), nh, slots, width),
        out_shape=(out, out),
        in_specs=[anywhere, anywhere, vmem, anywhere, anywhere, anywhere],
        out_specs=(vmem, vmem),
        scratch_shapes=[
            pltpu.VMEM((model, 2 * units), BF16),
            pltpu.VMEM((model, 2 * units), BF16),
            pltpu.VMEM((2 * units, model), BF16),
            pltpu.VMEM((2, 8, tokens), F32),
            pltpu.VMEM((2, nh, tokens, width), BF16),
            pltpu.VMEM((2, 2, nh, tokens, width), BF16),
            pltpu.VMEM((2, nh, nh, slots, width), BF16),
            pltpu.VMEM((2, nh, nh, slots, width), BF16),
            pltpu.VMEM((2, 2, nh, nh, slots, width), BF16),
            pltpu.VMEM((2, 3, nh, nh, slots, width), BF16),
            pltpu.VMEM((2, nh, tokens, width), BF16),
            pltpu.VMEM((2, 3, nh * slots, tokens), BF16),
            pltpu.VMEM((2, 3, 2, tokens, nh * slots), BF16),
            pltpu.VMEM((nh * slots, 2 * units), F32),
            pltpu.VMEM((nh * slots, 2 * units), F32),
            pltpu.VMEM((nh * slots, 2 * units), BF16),
            dma((3,)), dma((3,)), dma((3,)), dma, dma((2,)),
            dma((2, nh)), dma((2, nh)), dma((2, nh)), dma((2, 2, nh)),
            dma((2, 3, nh, nh)), dma((2, 2, nh, nh)), dma((2, 2, nh, nh)), dma((2, 3, nh, nh)),
            dma((2, 2, nh)), dma((2, nh)),
        ],
        compiler_params=pltpu.CompilerParams(
            collective_id=0, has_side_effects=True, vmem_limit_bytes=63 * 1024 * 1024
        ),
        cost_estimate=pl.CostEstimate(
            flops=12 * experts * cap * model * 2 * units,
            bytes_accessed=12 * model * units + 8 * tokens * model,
            transcendentals=0,
        ),
    )(act_fwd, act_rev, meta, w_gate, w_up, w_down)


def solution(mesh):
    return jax.shard_map(
        body,
        mesh=mesh,
        in_specs=(
            P("section", "expert", None),
            P("section", "expert", None),
            P("section", "expert", None),
            P("section", "expert", None),
            P("section", "expert", None),
            P("section", "expert", None),
            P("section", None, "expert"),
            P("section", None, "expert"),
            P("section", "expert", None),
        ),
        out_specs=(P("section", "expert", None), P("section", "expert", None)),
        check_vma=False,
    )
```

```python
import functools

import jax
import jax.numpy as jnp
from jax import lax
from jax.experimental import pallas as pl
from jax.experimental.pallas import tpu as pltpu
from jax.sharding import PartitionSpec as P

MESH = pl.DeviceIdType.MESH
F32 = jnp.float32
BF16 = jnp.bfloat16


def kernel(
    sections, nh, slots, width,
    act_f, act_r, meta_here, w_gate, w_up, w_down,
    out_f, out_r,
    wg, wu, wd, meta_there, arrived, raw, out_own, out_proxy, received, returned, part, pick, comb,
    acc_g, acc_u, hidden,
    w_local, w_send, w_recv, meta_send, meta_recv, relay_send, relay_recv, raw_send, raw_recv,
    disp_send, disp_recv, ret_send, ret_recv, part_send, part_recv,
):
    half_units = w_gate.shape[-1]
    tokens = arrived.shape[2]
    nq = nh // 2
    section = lax.axis_index("section")
    me = lax.axis_index("expert")
    core = lax.rem(me, 2)
    chip = me // 2
    half = chip // nh
    loc = lax.rem(chip, nh)
    pos = lax.rem(loc, nq)
    mid = (loc // nq) == (1 - half)
    my_q = jnp.where(mid, 0, 1)
    first_mid = nq * (1 - half)

    def at_chip(c):
        return (section, c * 2 + core)

    def in_half(offset):
        return at_chip(half * nh + lax.rem(loc + offset + nh, nh))

    def mid_peer(j):
        return at_chip(half * nh + first_mid + j)

    proxy = at_chip((1 - half) * nh + nq * half + pos)
    sources = (proxy, at_chip((1 - half) * nh + nq * (1 - half) + pos))
    other_core = (section, chip * 2 + 1 - core)
    after = (lax.rem(section + 1, sections), me)
    before = (lax.rem(section + sections - 1, sections), me)
    acts, outs, ways = (act_f, act_r), (out_f, out_r), (after, before)

    def columns(c):
        return pl.ds(pl.multiple_of(c * width, width), width)

    def remote(src, dst, send, recv, device):
        return pltpu.make_async_remote_copy(
            src_ref=src, dst_ref=dst, send_sem=send, recv_sem=recv,
            device_id=device, device_id_type=MESH,
        )

    def relay(st, c):
        return remote(acts[st].at[0, :, columns(c)], arrived.at[st, c],
                      relay_send.at[st, c], relay_recv.at[st, c], ways[st])

    def to_proxy(st, c, q):
        return remote(arrived.at[st, c], raw.at[st, q, c],
                      raw_send.at[st, c], raw_recv.at[st, q, c], proxy)

    def send_own(st, c, k):
        return remote(out_own.at[st, c, k], received.at[st, 0, c, k],
                      disp_send.at[st, 0, c, k], disp_recv.at[st, 0, c, k], in_half(k))

    def send_proxied(st, q, c, k, block):
        return remote(out_proxy.at[q, c, k], received.at[st, 1, c, block],
                      disp_send.at[st, 1 + q, c, k], disp_recv.at[st, 1, c, block], in_half(k))

    def return_own(st, c, k):
        return remote(received.at[st, 0, c, k], returned.at[st, 0, c, k],
                      ret_send.at[st, 0, c, k], ret_recv.at[st, 0, c, k], in_half(-k))

    def return_proxied(st, q, c, j, k):
        block = 2 * j + q
        return remote(received.at[st, 1, c, block], returned.at[st, 1 + q, c, k],
                      ret_send.at[st, 1, c, block], ret_recv.at[st, 1 + q, c, k], mid_peer(j))

    def from_proxy(st, q, c):
        return remote(raw.at[st, q, c], part.at[st, c],
                      part_send.at[st, q, c], part_recv.at[st, c], sources[q])

    def meta_copy(q):
        return remote(meta_here, meta_there.at[q], meta_send, meta_recv.at[q], proxy)

    barrier = pltpu.get_barrier_semaphore()
    greeted = [after, before, proxy, other_core] + [in_half(k) for k in range(1, nh)]
    for device in greeted:
        pl.semaphore_signal(barrier, inc=1, device_id=device, device_id_type=MESH)

    @pl.when(mid)
    def _():
        for device in sources:
            pl.semaphore_signal(barrier, inc=1, device_id=device, device_id_type=MESH)

    pl.semaphore_wait(barrier, len(greeted) + jnp.where(mid, 2, 0))

    for c in range(2):
        relay(0, c).start()

    meta_copy(my_q).start()

    here, there = pl.ds(0, half_units), pl.ds(half_units, half_units)
    places = ((w_gate, wg.at[:, here], wg.at[:, there]), (w_up, wu.at[:, here], wu.at[:, there]),
              (w_down, wd.at[here, :], wd.at[there, :]))
    local_copies, core_copies = [], []
    for i, (w, mine, theirs) in enumerate(places):
        local_copies.append(pltpu.make_async_copy(w.at[0], mine, w_local.at[i]))
        core_copies.append(remote(w.at[0], theirs, w_send.at[i], w_recv.at[i], other_core))
        local_copies[i].start()
        core_copies[i].start()

    row = lax.broadcasted_iota(jnp.int32, (tokens, tokens), 0)
    col = lax.broadcasted_iota(jnp.int32, (tokens, tokens), 1)
    earlier = jnp.where(row < col, 1.0, 0.0).astype(BF16)
    turn = loc + lax.broadcasted_iota(jnp.int32, (8, tokens), 0)
    expert = (half * nh + jnp.where(turn >= nh, turn - nh, turn)).astype(F32)
    slot_id = lax.broadcasted_iota(jnp.int32, (slots, tokens), 0).astype(F32)

    def tables(meta, p):
        for st in range(2):
            i0, i1 = meta[2 * st:2 * st + 1, :], meta[2 * st + 1:2 * st + 2, :]
            p0, p1 = meta[4 + 2 * st:5 + 2 * st, :], meta[5 + 2 * st:6 + 2 * st, :]
            total = p0 + p1
            first, second = i0 == expert, i1 == expert
            named = jnp.where(first, 1.0, jnp.where(second, 1.0, 0.0))
            gate = jnp.where(first, p0 / total, jnp.where(second, p1 / total, 0.0))
            rank = jnp.dot(named.astype(BF16), earlier, preferred_element_type=F32)
            slot = jnp.where(named > 0.5, rank, -1.0)
            weighted = []
            for k in range(nh):
                chosen = jnp.where(slot_id == slot[k:k + 1, :], 1.0, 0.0)
                pick[st, p, pl.ds(k * slots, slots), :] = chosen.astype(BF16)
                weighted.append(chosen * gate[k:k + 1, :])
            flat = jnp.concatenate(weighted, axis=0).T
            top = flat.astype(BF16)
            comb[st, p, 0] = top
            comb[st, p, 1] = (flat - top.astype(F32)).astype(BF16)

    def own(st, c):
        relay(st, c).wait_recv()
        to_proxy(st, c, my_q).start()
        if st == 0:
            @pl.when(c < nh - 2)
            def _():
                relay(0, c + 2).start()

            @pl.when(c >= nh - 2)
            def _():
                relay(1, c - (nh - 2)).start()

        rows = jnp.dot(pick[st, 0], arrived[st, c], preferred_element_type=F32).astype(BF16)
        received[st, 0, c, 0] = rows[:slots]
        for k in range(1, nh):
            out_own[st, c, k] = rows[k * slots:(k + 1) * slots]
            send_own(st, c, k).start()

    def proxied(st, c):
        for q in range(2):
            to_proxy(st, c, q).wait_recv()
            rows = jnp.dot(pick[st, 1 + q], raw[st, q, c], preferred_element_type=F32).astype(BF16)
            received[st, 1, c, 2 * pos + q] = rows[:slots]
            for k in range(1, nh):
                if st == 1:
                    send_proxied(0, q, c, k, 2 * pos + q).wait_send()
                out_proxy[q, c, k] = rows[k * slots:(k + 1) * slots]
                send_proxied(st, q, c, k, 2 * pos + q).start()

    def experts(st, g):
        acc_g[...] = jnp.zeros_like(acc_g)
        acc_u[...] = jnp.zeros_like(acc_u)

        @pl.loop(0, nh)
        def _(c):
            if g == 0:
                for k in range(1, nh):
                    send_own(st, c, k).wait_recv()
            else:
                for j in range(nq):
                    @pl.when(jnp.logical_not(mid & (pos == j)))
                    def _():
                        for q in range(2):
                            send_proxied(st, q, c, 1, 2 * j + q).wait_recv()

            x = received[st, g, c].reshape(nh * slots, width)
            acc_g[...] += jnp.dot(x, wg[columns(c), :], preferred_element_type=F32)
            acc_u[...] += jnp.dot(x, wu[columns(c), :], preferred_element_type=F32)

        gate = acc_g[...]
        hidden[...] = (gate / (1.0 + jnp.exp(-gate)) * acc_u[...]).astype(BF16)

        @pl.loop(0, nh)
        def _(c):
            y = jnp.dot(hidden[...], wd[:, columns(c)], preferred_element_type=F32).astype(BF16)
            if g == 0:
                returned[st, 0, c, 0] = y[:slots]
                for k in range(1, nh):
                    received[st, 0, c, k] = y[k * slots:(k + 1) * slots]
                    return_own(st, c, k).start()
            else:
                for j in range(nq):
                    blocks = [y[(2 * j + q) * slots:(2 * j + q + 1) * slots] for q in range(2)]
                    myself = mid & (pos == j)

                    @pl.when(myself)
                    def _():
                        for q in range(2):
                            returned[st, 1 + q, c, 0] = blocks[q]

                    @pl.when(jnp.logical_not(myself))
                    def _():
                        offset = lax.rem(loc - first_mid - j + nh, nh)
                        for q in range(2):
                            received[st, 1, c, 2 * j + q] = blocks[q]
                            return_proxied(st, q, c, j, offset).start()

    def weighted_sum(st, p, c):
        rows = returned[st, p, c].reshape(nh * slots, width)
        return (jnp.dot(comb[st, p, 0], rows, preferred_element_type=F32)
                + jnp.dot(comb[st, p, 1], rows, preferred_element_type=F32))

    def proxy_sum(st, c):
        for q in range(2):
            for k in range(1, nh):
                return_proxied(st, q, c, 0, k).wait_recv()
            raw[st, q, c] = weighted_sum(st, 1 + q, c).astype(BF16)
            from_proxy(st, q, c).start()

    def finish(st, c):
        for k in range(1, nh):
            return_own(st, c, k).wait_recv()
        total = arrived[st, c].astype(F32) + weighted_sum(st, 0, c)
        from_proxy(st, 0, c).wait_recv()
        outs[st][0, :, columns(c)] = (total + part[st, c].astype(F32)).astype(BF16)

    tables(meta_here[...], 0)

    @pl.loop(0, nh)
    def _(c):
        own(0, c)

    @pl.loop(2, nh)
    def _(c):
        relay(1, c).start()

    @pl.when(mid)
    def _():
        for q in range(2):
            meta_copy(q).wait_recv()
            tables(meta_there[q], 1 + q)

        @pl.loop(0, nh)
        def _(c):
            proxied(0, c)

        @pl.loop(0, nh)
        def _(c):
            own(1, c)

    for i in range(3):
        local_copies[i].wait()
        core_copies[i].wait_recv()

    experts(0, 0)

    @pl.when(jnp.logical_not(mid))
    def _():
        @pl.loop(0, nh)
        def _(c):
            own(1, c)

    experts(0, 1)

    @pl.when(mid)
    def _():
        @pl.loop(0, nh)
        def _(c):
            proxied(1, c)

    experts(1, 0)

    @pl.when(mid)
    def _():
        @pl.loop(0, nh)
        def _(c):
            proxy_sum(0, c)

    experts(1, 1)

    @pl.when(mid)
    def _():
        @pl.loop(0, nh)
        def _(c):
            proxy_sum(1, c)

    @pl.loop(0, nh)
    def _(c):
        finish(0, c)

    @pl.loop(0, nh)
    def _(c):
        finish(1, c)

    meta_copy(my_q).wait_send()
    for i in range(3):
        core_copies[i].wait_send()

    @pl.loop(0, nh)
    def _(c):
        for st in range(2):
            relay(st, c).wait_send()
            to_proxy(st, c, my_q).wait_send()
            for k in range(1, nh):
                send_own(st, c, k).wait_send()
                return_own(st, c, k).wait_send()
            for j in range(nq):
                @pl.when(jnp.logical_not(mid & (pos == j)))
                def _():
                    for q in range(2):
                        return_proxied(st, q, c, j, 1).wait_send()

    @pl.when(mid)
    def _():
        @pl.loop(0, nh)
        def _(c):
            for q in range(2):
                for st in range(2):
                    from_proxy(st, q, c).wait_send()
                for k in range(1, nh):
                    send_proxied(1, q, c, k, 2 * pos + q).wait_send()


def body(act_fwd, act_rev, ids_fwd, ids_rev, probs_fwd, probs_rev, w_gate, w_up, w_down):
    tokens, top = ids_fwd.shape[1:]
    model = act_fwd.shape[2]
    units = w_gate.shape[2]
    experts = lax.axis_size("expert") // 2
    nh = experts // 2
    width = model // nh
    cap = 2 * (3 * tokens * top // (4 * experts))
    slots = -(-cap // 16) * 16
    meta = jnp.concatenate(
        [ids_fwd[0].astype(F32), ids_rev[0].astype(F32), probs_fwd[0], probs_rev[0]], axis=1
    ).T
    anywhere = pl.BlockSpec(memory_space=pl.ANY)
    vmem = pl.BlockSpec(memory_space=pltpu.VMEM)
    dma = pltpu.SemaphoreType.DMA
    out = jax.ShapeDtypeStruct((1, tokens, model), BF16)
    return pl.pallas_call(
        functools.partial(kernel, lax.axis_size("section"), nh, slots, width),
        out_shape=(out, out),
        in_specs=[anywhere, anywhere, vmem, anywhere, anywhere, anywhere],
        out_specs=(vmem, vmem),
        scratch_shapes=[
            pltpu.VMEM((model, 2 * units), BF16),
            pltpu.VMEM((model, 2 * units), BF16),
            pltpu.VMEM((2 * units, model), BF16),
            pltpu.VMEM((2, 8, tokens), F32),
            pltpu.VMEM((2, nh, tokens, width), BF16),
            pltpu.VMEM((2, 2, nh, tokens, width), BF16),
            pltpu.VMEM((2, nh, nh, slots, width), BF16),
            pltpu.VMEM((2, nh, nh, slots, width), BF16),
            pltpu.VMEM((2, 2, nh, nh, slots, width), BF16),
            pltpu.VMEM((2, 3, nh, nh, slots, width), BF16),
            pltpu.VMEM((2, nh, tokens, width), BF16),
            pltpu.VMEM((2, 3, nh * slots, tokens), BF16),
            pltpu.VMEM((2, 3, 2, tokens, nh * slots), BF16),
            pltpu.VMEM((nh * slots, 2 * units), F32),
            pltpu.VMEM((nh * slots, 2 * units), F32),
            pltpu.VMEM((nh * slots, 2 * units), BF16),
            dma((3,)), dma((3,)), dma((3,)), dma, dma((2,)),
            dma((2, nh)), dma((2, nh)), dma((2, nh)), dma((2, 2, nh)),
            dma((2, 3, nh, nh)), dma((2, 2, nh, nh)), dma((2, 2, nh, nh)), dma((2, 3, nh, nh)),
            dma((2, 2, nh)), dma((2, nh)),
        ],
        compiler_params=pltpu.CompilerParams(
            collective_id=0, has_side_effects=True, vmem_limit_bytes=63 * 1024 * 1024
        ),
        cost_estimate=pl.CostEstimate(
            flops=12 * experts * cap * model * 2 * units,
            bytes_accessed=12 * model * units + 8 * tokens * model,
            transcendentals=0,
        ),
    )(act_fwd, act_rev, meta, w_gate, w_up, w_down)


def solution(mesh):
    return jax.shard_map(
        body,
        mesh=mesh,
        in_specs=(
            P("section", "expert", None),
            P("section", "expert", None),
            P("section", "expert", None),
            P("section", "expert", None),
            P("section", "expert", None),
            P("section", "expert", None),
            P("section", None, "expert"),
            P("section", None, "expert"),
            P("section", "expert", None),
        ),
        out_specs=(P("section", "expert", None), P("section", "expert", None)),
        check_vma=False,
    )
```
